32 devices in a mesh: depth: 4 (over z), rows: 8 (over y, x, core).
Axes of the slice: x: 2, y: 2, z: 4, core: 2. Of those that a mesh axis runs over, the one named last changes fastest.
Arguments:
- in_flight: float32 [4, 2, 1024, 1024], P('depth', None, 'rows'), may hold values from -6 to 6
- phase_index: bfloat16 [8, 1024, 1024], P('depth', 'rows'), may hold values from -2 to 2
- absorption: bfloat16 [8, 1024, 1024], P('depth', 'rows'), may hold values from 0.099609375 to 2
Outputs:
- exits: float32 [4, 2, 1024, 1024], P('depth', None, 'rows')
The draws below stay inside these ranges and needn't reach their ends.
All inputs are finite; a program needn't handle non-finite values.
Results may differ from the reference program's by a relative error of at most 0.0003.
Values may be sent and summed in bfloat16 or wider, within the bound.
No kernel may reach another device: no remote copies, remote signals or barrier semaphores. Data moves between devices by JAX's collectives and lax.ppermute only.
A program may use at most 64 MiB of HBM per device.

```python
import math
import jax
import jax.numpy as jnp
from jax import lax

NXY = 1024
SLICES = 2
TAYLOR = 4
TICKS = 2
GROUPS = 4
LAYERS = 8


def level_of(rng, extent, pieces, smallest, largest):
    def one(axis_at, shards_of):
        heights = jax.random.uniform(jax.random.fold_in(jax.random.fold_in(rng, 6), axis_at), (shards_of,), jnp.float32, smallest / len(pieces), largest / len(pieces))
        return jnp.repeat(jnp.exp(heights), extent[axis_at] // shards_of).reshape((-1,) + (1,) * (len(extent) - axis_at - 1))

    loudness = one(*pieces[0])
    for cut in pieces[1:]:
        loudness = loudness * one(*cut)
    return loudness


def bell_draw(rng, extent, deviation, reach, split=(), kind=jnp.bfloat16):
    gain = level_of(rng, extent, split, -0.22, 0.18) if split else 1.0
    array = jax.random.normal(rng, extent, jnp.float32) * deviation * gain
    return jnp.minimum(jnp.maximum(array, -reach), reach).astype(kind)


def setup_inputs(seed: int = 0) -> dict:
    key_of = jax.random.split(jax.random.key(seed), 4)
    in_flight = bell_draw(key_of[0], (GROUPS, 2, NXY, NXY), 1.0, 6.0, ((0, 4), (2, 8)), jnp.float32)
    phase_index = bell_draw(key_of[1], (LAYERS, NXY, NXY), 0.5, 2.0, ((0, 4), (1, 8)))
    absorption = jnp.clip(jnp.exp(math.log(2.0) - 2.9996462 * jax.random.uniform(key_of[2], (LAYERS, NXY, NXY), jnp.float32) ** level_of(key_of[2], (LAYERS, NXY, NXY), ((0, 4), (1, 8)), -0.2, 0.2)), 0.099609375, 2.0).astype(jnp.bfloat16)
    return {"in_flight": in_flight, "phase_index": phase_index, "absorption": absorption}


lateral = 0.22
contrast = 0.2


def laplace(values):
    padded = jnp.pad(values, ((0, 0), (1, 1), (1, 1)))
    return padded[:, 2:, 1:-1] + padded[:, :-2, 1:-1] + padded[:, 1:-1, 2:] + padded[:, 1:-1, :-2] - 4.0 * values


def generator(values, index_part, loss_part):
    stirred = lateral * laplace(values) + contrast * index_part * values
    damping = contrast * loss_part
    return jnp.stack([-stirred[1] - damping * values[0], stirred[0] - damping * values[1]])


def slice_step(values, index_part, loss_part):
    summed = values
    term_now = values
    for degree in range(1, TAYLOR + 1):
        term_now = generator(term_now, index_part, loss_part) / degree
        summed = summed + term_now
    return summed


def fresnel(length):
    frequency = jnp.arange(length, dtype=jnp.int32)
    frequency = jnp.where(frequency < length // 2, frequency, frequency - length)
    phase_angle = ((frequency * frequency) % (8 * length)).astype(jnp.float32) * (math.pi / (4 * length))
    return lax.complex(jnp.cos(phase_angle), -jnp.sin(phase_angle))


def gap(values):
    spectrum = jnp.fft.fft2(lax.complex(values[0], values[1]))
    kernel = fresnel(NXY)
    spectrum = spectrum * kernel[:, None] * kernel[None, :]
    result = jnp.fft.ifft2(spectrum)
    return jnp.stack([jnp.real(result), jnp.imag(result)])


def group_pass(inputs):
    values, deltas, absorbs = inputs
    for slice_index in range(SLICES):
        values = slice_step(values, deltas[slice_index].astype(jnp.float32), absorbs[slice_index].astype(jnp.float32))
    return gap(values)


def reference(in_flight, phase_index, absorption):
    deltas = phase_index.reshape(GROUPS, SLICES, NXY, NXY)
    absorbs = absorption.reshape(GROUPS, SLICES, NXY, NXY)
    fields = in_flight
    for tick_index in range(TICKS):
        if tick_index > 0:
            fields = jnp.roll(fields, 1, axis=0)
        fields = lax.map(group_pass, (fields, deltas, absorbs))
    return fields
```

```python
import functools
import math

import jax
import jax.numpy as jnp
import ml_dtypes
import numpy as np
from jax import lax
from jax.experimental import pallas as pl
from jax.experimental.pallas import tpu as pltpu
from jax.sharding import PartitionSpec as P

TAYLOR = 4
LATERAL = 0.22
CONTRAST = 0.2
LANES = 128
VMEM_BYTES = 48 * 1024 * 1024
F32 = jnp.float32
BF16 = jnp.bfloat16


def gap_tables(length):
    frequency = np.arange(length)
    frequency = np.where(frequency < length // 2, frequency, frequency - length)
    response = np.exp(-1j * math.pi * (frequency * frequency % (8 * length)) / (4 * length))
    spread = np.fft.ifft(response)
    half = length // 2
    lag = np.arange(half)[:, None] - np.arange(half)[None, :]
    near, far = spread[lag % length], spread[(lag + half) % length]
    even, odd = (near + far) / 2, (near - far) / 2
    table = np.stack([even.real, even.imag, odd.real, odd.imag]).astype(np.float32)
    high = table.astype(ml_dtypes.bfloat16)
    low = (table - high.astype(np.float32)).astype(ml_dtypes.bfloat16)
    return np.stack([high, low])


def split(values):
    high = values.astype(BF16)
    return high, (values - high.astype(F32)).astype(BF16)


def product(tables, which, operand, transposed):
    high, low = operand

    def dot(part, data):
        table = tables[part, which]
        if transposed:
            return lax.dot_general(table, data, (((1,), (1,)), ((), ())), preferred_element_type=F32)
        return lax.dot_general(data, table, (((1,), (0,)), ((), ())), preferred_element_type=F32)

    return dot(0, high) + (dot(1, high) + dot(0, low))


def half_gap(tables, first, stacked, rows, transposed):
    operand = split(stacked)
    by_re = product(tables, first, operand, transposed)
    by_im = product(tables, first + 1, operand, transposed)
    if transposed:
        return (by_re[:, :rows] - by_im[:, rows:], by_re[:, rows:] + by_im[:, :rows])
    return (by_re[:rows] - by_im[rows:], by_re[rows:] + by_im[:rows])


def gap_transposed(tables, field, rows):
    half = field.shape[1] // 2
    left, right = field[:, :half], field[:, half:]
    even = half_gap(tables, 0, left + right, rows, True)
    odd = half_gap(tables, 2, left - right, rows, True)
    return [(even[0] + odd[0], even[1] + odd[1]), (even[0] - odd[0], even[1] - odd[1])]


def gap_from_blocks(tables, blocks_ref, rows):
    count = blocks_ref.shape[0] // 2

    def folded(sign):
        def part(lane):
            return jnp.concatenate(
                [
                    blocks_ref[i, :, lane : lane + LANES]
                    + sign * blocks_ref[i + count, :, lane : lane + LANES]
                    for i in range(count)
                ],
                axis=1,
            )

        return jnp.concatenate([part(0), part(LANES)], axis=0)

    even = half_gap(tables, 0, folded(1.0), rows, False)
    odd = half_gap(tables, 2, folded(-1.0), rows, False)
    return [(even[0] + odd[0], even[1] + odd[1]), (even[0] - odd[0], even[1] - odd[1])]


def apply_slices(count, inside, load_coefficients, bufs, phase, loss, length):
    tall = phase.shape[0]
    groups = tall // 8
    base = bufs[0]

    def step(source, target, weight, keep_halo):
        def group(index, flag=None):
            row = index * 8
            if not isinstance(index, int):
                row = pl.multiple_of(row, 8)
            mid = pl.ds(row + 8, 8)
            here = pl.ds(row, 8)
            gather, centre = [], []
            for part in range(2):
                cell = source[part, mid, :]
                width = cell.shape[1]
                around = source.at[part, pl.ds(row, 24)]
                total = (
                    around[7:15, :length]
                    + around[9:17, :length]
                    + pltpu.roll(cell, 1, 1)[:, :length]
                    + pltpu.roll(cell, width - 1, 1)[:, :length]
                )
                cell = cell[:, :length]
                gather.append(total + phase[here, :] * cell)
                centre.append(cell)
            damp = loss[here, :]
            new_re = base[0, mid, :length] - weight * (gather[1] + damp * centre[0])
            new_im = base[1, mid, :length] + weight * (gather[0] - damp * centre[1])
            if flag is not None:
                new_re = jnp.where(flag, new_re, 0.0)
                new_im = jnp.where(flag, new_im, 0.0)
            target[0, mid, :length] = new_re
            target[1, mid, :length] = new_im

        if keep_halo:
            group(0, inside[0])
            group(groups - 1, inside[1])

        def body(index, carry):
            group(index)
            return carry

        lax.fori_loop(1, groups - 1, body, 0)

    for slice_index in range(count):
        load_coefficients(slice_index)
        source = bufs[0]
        for degree in range(TAYLOR, 0, -1):
            target = bufs[0] if degree == 1 else bufs[1 + degree % 2]
            last = slice_index == count - 1 and degree == 1
            step(source, target, LATERAL / degree, not last)
            source = target


def scaled_phase(values):
    return values.astype(F32) * (CONTRAST / LATERAL) - 4.0


def scaled_loss(values):
    return values.astype(F32) * (CONTRAST / LATERAL)


def clear_margins(bufs, length):
    for buf in bufs:
        buf[:, :, length:] = jnp.zeros(buf.shape[:2] + (buf.shape[2] - length,), F32)


def first_kernel(
    height, count, width, edge_ref, field, above, below, index_ref, loss_ref, tables, out,
    buf0, buf1, buf2, phase, loss, spectrum,
):
    bufs = (buf0, buf1, buf2)
    length = field.shape[2]
    clear_margins(bufs, length)
    buf0[:, 8 : 8 + width, :length] = above[0:2]
    buf0[:, 8 + width : 8 + width + height, :length] = field[...]
    buf0[:, 8 + width + height : 8 + 2 * width + height, :length] = below[0:2]

    def load_coefficients(k):
        phase[0:width, :] = scaled_phase(above[2 + k])
        loss[0:width, :] = scaled_loss(above[2 + count + k])
        for row in range(0, height, 16):
            phase[width + row : width + row + 16, :] = scaled_phase(index_ref[k, row : row + 16, :])
            loss[width + row : width + row + 16, :] = scaled_loss(loss_ref[k, row : row + 16, :])
        phase[width + height :, :] = scaled_phase(below[2 + k])
        loss[width + height :, :] = scaled_loss(below[2 + count + k])

    inside = (edge_ref[0] > 0, edge_ref[1] > 0)
    apply_slices(count, inside, load_coefficients, bufs, phase, loss, length)
    core = buf0[:, 8 + width : 8 + width + height, :length]
    halves = gap_transposed(tables, core.reshape(2 * height, length), height)
    half = length // 2
    spectrum[0:width, :] = jnp.zeros((width, 2 * height), F32)
    spectrum[width + length :, :] = jnp.zeros((width, 2 * height), F32)
    for which, (real, imag) in enumerate(halves):
        start = width + which * half
        spectrum[start : start + half, :height] = real
        spectrum[start : start + half, height:] = imag
    for k in range(out.shape[0]):
        out[k] = spectrum[k * height : k * height + height + 2 * width, :]


def second_kernel(
    height, count, width, edge_ref, blocks, specimen, tables, out, buf0, buf1, buf2, phase, loss,
):
    bufs = (buf0, buf1, buf2)
    tall = height + 2 * width
    length = specimen.shape[2]
    half = length // 2
    clear_margins(bufs, length)
    for which, (real, imag) in enumerate(gap_from_blocks(tables, blocks, tall)):
        buf0[0, 8 : 8 + tall, which * half : (which + 1) * half] = real
        buf0[1, 8 : 8 + tall, which * half : (which + 1) * half] = imag

    def load_coefficients(k):
        for row in range(0, tall, 16):
            phase[row : row + 16, :] = scaled_phase(specimen[k, row : row + 16, :])
            loss[row : row + 16, :] = scaled_loss(specimen[count + k, row : row + 16, :])

    inside = (edge_ref[0] > 0, edge_ref[1] > 0)
    apply_slices(count, inside, load_coefficients, bufs, phase, loss, length)
    core = buf0[:, 8 + width : 8 + width + height, :length]
    for which, (real, imag) in enumerate(
        gap_transposed(tables, core.reshape(2 * height, length), height)
    ):
        out[which * half : (which + 1) * half, :height] = real
        out[which * half : (which + 1) * half, height:] = imag


def third_kernel(height, blocks, tables, out):
    half = out.shape[2] // 2
    for which, (real, imag) in enumerate(gap_from_blocks(tables, blocks, height)):
        out[0, :, which * half : (which + 1) * half] = real
        out[1, :, which * half : (which + 1) * half] = imag


VMEM = pl.BlockSpec(memory_space=pltpu.VMEM)
SMEM = pl.BlockSpec(memory_space=pltpu.SMEM)


def call(kernel, in_specs, out_shape, scratch, name, flops, moved):
    return pl.pallas_call(
        kernel,
        in_specs=in_specs,
        out_specs=VMEM,
        out_shape=out_shape,
        scratch_shapes=scratch,
        compiler_params=pltpu.CompilerParams(vmem_limit_bytes=VMEM_BYTES),
        cost_estimate=pl.CostEstimate(flops=flops, bytes_accessed=moved, transcendentals=0),
        name=name,
    )


def in_lane_blocks(pieces):
    sources, rows, both = pieces.shape
    own = both // 2
    if own == LANES:
        return pieces
    joined = pieces.reshape(sources, rows, 2, own).transpose(1, 2, 0, 3)
    joined = joined.reshape(rows, 2, sources * own // LANES, LANES).transpose(2, 0, 1, 3)
    return joined.reshape(sources * own // LANES, rows, 2 * LANES)


def to_others(pieces):
    return lax.all_to_all(pieces, "rows", split_axis=0, concat_axis=0, tiled=True)


def local(in_flight, phase_index, absorption):
    field = in_flight[0]
    count, height, length = phase_index.shape
    slabs = lax.axis_size("rows")
    groups = lax.axis_size("depth")
    width = count * TAYLOR
    tall = height + 2 * width
    place = lax.axis_index("rows")
    edge = jnp.stack([(place > 0), (place < slabs - 1)]).astype(jnp.int32)
    tables = jnp.asarray(gap_tables(length))

    def lines(start):
        def cut(array):
            return lax.slice_in_dim(array, start, start + width, axis=1).astype(F32)

        return jnp.concatenate([cut(field), cut(phase_index), cut(absorption)], axis=0)

    down = [(i, i + 1) for i in range(slabs - 1)]
    up = [(i + 1, i) for i in range(slabs - 1)]
    above = lax.ppermute(lines(height - width), "rows", down)
    below = lax.ppermute(lines(0), "rows", up)

    turned = jnp.concatenate([phase_index, absorption], axis=0).transpose(0, 2, 1)
    turned = jnp.pad(turned, ((0, 0), (width, width), (0, 0)))
    turned = jnp.stack(
        [lax.slice_in_dim(turned, k * height, k * height + tall, axis=1) for k in range(slabs)]
    )
    turned = to_others(turned)
    specimen = turned.transpose(1, 2, 0, 3).reshape(2 * count, tall, length)

    buffer = pltpu.VMEM((2, tall + 16, length + LANES), F32)
    coefficient = pltpu.VMEM((tall, length), F32)
    slice_flops = 40 * count * TAYLOR * tall * length
    gap_flops = 24 * height * length * length // 2
    pieces = call(
        functools.partial(first_kernel, height, count, width),
        [SMEM] + [VMEM] * 6,
        jax.ShapeDtypeStruct((slabs, tall, 2 * height), F32),
        [buffer] * 3 + [coefficient] * 2 + [pltpu.VMEM((length + 2 * width, 2 * height), F32)],
        "slices_and_gap_rows",
        slice_flops + gap_flops,
        8 * 1024 * 1024,
    )(edge, field, above, below, phase_index, absorption, tables)

    pieces = lax.ppermute(pieces, "depth", [(g, (g + 1) % groups) for g in range(groups)])
    blocks = in_lane_blocks(to_others(pieces))

    pieces = call(
        functools.partial(second_kernel, height, count, width),
        [SMEM] + [VMEM] * 3,
        jax.ShapeDtypeStruct((length, 2 * height), F32),
        [buffer] * 3 + [coefficient] * 2,
        "gap_slices_gap_columns",
        slice_flops + 2 * gap_flops,
        8 * 1024 * 1024,
    )(edge, blocks, specimen, tables)

    blocks = in_lane_blocks(to_others(pieces.reshape(slabs, height, 2 * height)))

    field = call(
        functools.partial(third_kernel, height),
        [VMEM] * 2,
        jax.ShapeDtypeStruct((2, height, length), F32),
        [],
        "gap_rows",
        gap_flops,
        6 * 1024 * 1024,
    )(blocks, tables)
    return field[None]


def solution(mesh):
    placed = (P("depth", None, "rows", None), P("depth", "rows", None), P("depth", "rows", None))
    return jax.shard_map(
        local, mesh=mesh, in_specs=placed, out_specs=P("depth", None, "rows", None), check_vma=False
    )
```

```python
import functools
import math

import jax
import jax.numpy as jnp
import ml_dtypes
import numpy as np
from jax import lax
from jax.experimental import pallas as pl
from jax.experimental.pallas import tpu as pltpu
from jax.sharding import PartitionSpec as P

TAYLOR = 4
LATERAL = 0.22
CONTRAST = 0.2
LANES = 128
VMEM_BYTES = 48 * 1024 * 1024
F32 = jnp.float32
BF16 = jnp.bfloat16


def gap_tables(length):
    frequency = np.arange(length)
    frequency = np.where(frequency < length // 2, frequency, frequency - length)
    response = np.exp(-1j * math.pi * (frequency * frequency % (8 * length)) / (4 * length))
    spread = np.fft.ifft(response)
    half = length // 2
    lag = np.arange(half)[:, None] - np.arange(half)[None, :]
    near, far = spread[lag % length], spread[(lag + half) % length]
    even, odd = (near + far) / 2, (near - far) / 2
    table = np.stack([even.real, even.imag, odd.real, odd.imag]).astype(np.float32)
    high = table.astype(ml_dtypes.bfloat16)
    low = (table - high.astype(np.float32)).astype(ml_dtypes.bfloat16)
    return np.stack([high, low])


FLOOR = 255.0
SPAN = 250.0
STEEP = SPAN / math.log2(1.0 + FLOOR)
SCALE_ROWS = 16


def scale_of(arrays):
    largest = functools.reduce(jnp.maximum, [jnp.max(jnp.abs(array)) for array in arrays])
    return jnp.maximum(largest * (1.0 + 2.0**-7), 1e-30).astype(BF16).astype(F32)


def encode(values, scale):
    level = jnp.log2(1.0 + jnp.abs(values) * (FLOOR / scale))
    code = jnp.exp2(level * STEEP - SPAN / 2)
    return jnp.where(values < 0, -code, code).astype(BF16)


def decode(codes, scale):
    codes = codes.astype(F32)
    level = (jnp.log2(jnp.abs(codes)) + SPAN / 2) * (1.0 / STEEP)
    values = (jnp.exp2(level) - 1.0) * (scale * (1.0 / FLOOR))
    return jnp.where(codes < 0, -values, values)


def decode_block(blocks_ref, i, lane, rows):
    lanes = slice(lane, lane + LANES)
    scale = blocks_ref[i, rows : rows + SCALE_ROWS, lanes].astype(F32)[0:1]
    return decode(blocks_ref[i, 0:rows, lanes], scale)


def split(values):
    high = values.astype(BF16)
    return high, (values - high.astype(F32)).astype(BF16)


def product(tables, which, operand, transposed):
    high, low = operand

    def dot(part, data):
        table = tables[part, which]
        if transposed:
            return lax.dot_general(table, data, (((1,), (1,)), ((), ())), preferred_element_type=F32)
        return lax.dot_general(data, table, (((1,), (0,)), ((), ())), preferred_element_type=F32)

    return dot(0, high) + (dot(1, high) + dot(0, low))


def half_gap(tables, first, stacked, rows, transposed):
    operand = split(stacked)
    by_re = product(tables, first, operand, transposed)
    by_im = product(tables, first + 1, operand, transposed)
    if transposed:
        return (by_re[:, :rows] - by_im[:, rows:], by_re[:, rows:] + by_im[:, :rows])
    return (by_re[:rows] - by_im[rows:], by_re[rows:] + by_im[:rows])


def gap_transposed(tables, field, rows):
    half = field.shape[1] // 2
    left, right = field[:, :half], field[:, half:]
    even = half_gap(tables, 0, left + right, rows, True)
    odd = half_gap(tables, 2, left - right, rows, True)
    return [(even[0] + odd[0], even[1] + odd[1]), (even[0] - odd[0], even[1] - odd[1])]


def gap_from_blocks(tables, blocks_ref, rows):
    count = blocks_ref.shape[0] // 2

    parts = [
        [decode_block(blocks_ref, i, lane, rows) for i in range(2 * count)] for lane in (0, LANES)
    ]

    def folded(sign):
        return jnp.concatenate(
            [
                jnp.concatenate([part[i] + sign * part[i + count] for i in range(count)], axis=1)
                for part in parts
            ],
            axis=0,
        )

    even = half_gap(tables, 0, folded(1.0), rows, False)
    odd = half_gap(tables, 2, folded(-1.0), rows, False)
    return [(even[0] + odd[0], even[1] + odd[1]), (even[0] - odd[0], even[1] - odd[1])]


def shifted(row):
    lane = lax.broadcasted_iota(jnp.int32, row[0].shape, 1)
    count = len(row)
    right = [pltpu.roll(cell, 1, 1) for cell in row]
    left = [pltpu.roll(cell, LANES - 1, 1) for cell in row]
    before = [
        jnp.where(lane == 0, right[i - 1] if i else 0.0, right[i]) for i in range(count)
    ]
    after = [
        jnp.where(lane == LANES - 1, left[i + 1] if i + 1 < count else 0.0, left[i])
        for i in range(count)
    ]
    return before, after


def spread_rows(natural, target, first):
    blocks, tall, _ = natural.shape
    steps = tall // 8
    for i in range(blocks):
        for k in range(steps):
            target[i, 8 * (k + first) : 8 * (k + first) + 8, :] = natural.at[i][
                pl.ds(k, 8, stride=steps), :
            ]


def gather_rows(source, first, natural):
    blocks, tall, _ = natural.shape
    steps = tall // 8
    for i in range(blocks):
        for k in range(steps):
            natural.at[i][pl.ds(k, 8, stride=steps), :] = source[
                i, 8 * (k + first) : 8 * (k + first) + 8, :
            ]


def wrap(buf, steps):
    for part in range(2):
        for i in range(buf.shape[1]):
            last = buf[part, i, 8 * steps : 8 * steps + 8, :]
            buf[part, i, 0:8, :] = pltpu.roll(last, 1, 0)
            initial = buf[part, i, 8:16, :]
            buf[part, i, 8 * steps + 8 : 8 * steps + 16, :] = pltpu.roll(initial, 7, 0)


def apply_slices(count, width, inside, load_coefficients, bufs, phase, loss, keep):
    blocks, tall, _ = phase.shape
    steps = tall // 8
    sublane = lax.broadcasted_iota(jnp.int32, (8, LANES), 0)
    for k in range(steps if inside else 0):
        row = sublane * steps + k
        top = jnp.logical_and(row < width, inside[0] == 0)
        bottom = jnp.logical_and(row >= tall - width, inside[1] == 0)
        keep[8 * k : 8 * k + 8, :] = jnp.where(jnp.logical_or(top, bottom), 0.0, 1.0)
    base = bufs[0]

    def step(source, target, weight):
        def body(k):
            def rows(ref, at, *lead):
                start = (k + at) * 8
                return [ref[lead + (i, pl.ds(start, 8), slice(None))] for i in range(blocks)]

            factor = keep[pl.ds(k * 8, 8), :] * weight if inside else weight
            phases = rows(phase, 0)
            losses = rows(loss, 0)
            here, total = [], []
            for part in range(2):
                cells = rows(source, 1, part)
                above, below = rows(source, 0, part), rows(source, 2, part)
                before, after = shifted(cells)
                here.append(cells)
                total.append(
                    [
                        (above[i] + below[i]) + (before[i] + after[i]) + phases[i] * cells[i]
                        for i in range(blocks)
                    ]
                )
            start = pl.ds((k + 1) * 8, 8)
            for i in range(blocks):
                target[0, i, start, :] = base[0, i, start, :] - factor * (
                    total[1][i] + losses[i] * here[0][i]
                )
                target[1, i, start, :] = base[1, i, start, :] + factor * (
                    total[0][i] - losses[i] * here[1][i]
                )

        for k in range(steps):
            body(k)
        wrap(target, steps)

    def one_slice(slice_index, carry):
        load_coefficients(slice_index)
        source = bufs[0]
        for degree in range(TAYLOR, 0, -1):
            target = bufs[0] if degree == 1 else bufs[1 + degree % 2]
            step(source, target, LATERAL / degree)
            source = target
        return carry

    lax.fori_loop(0, count, one_slice, 0)


def scaled_phase(values):
    return values.astype(F32) * (CONTRAST / LATERAL) - 4.0


def scaled_loss(values):
    return values.astype(F32) * (CONTRAST / LATERAL)


def by_blocks(target, start, values):
    rows = values.shape[0]
    for i in range(values.shape[1] // LANES):
        target[i, start : start + rows, :] = values[:, i * LANES : (i + 1) * LANES]


def joined(natural, start, rows):
    return jnp.concatenate(
        [
            jnp.concatenate(
                [natural[part, i, start : start + rows, :] for i in range(natural.shape[1])], axis=1
            )
            for part in range(2)
        ],
        axis=0,
    )


def lines_kernel(
    height, count, width, field, index_ref, loss_ref, head, tail, cells, deltas, absorbs, sems
):
    copies = []
    for end, start in enumerate((0, height - width)):
        copies.append((field.at[:, pl.ds(start, width)], cells.at[end]))
    for end, start in enumerate((0, height - 16)):
        copies.append((index_ref.at[:, pl.ds(start, 16)], deltas.at[end]))
        copies.append((loss_ref.at[:, pl.ds(start, 16)], absorbs.at[end]))
    started = [
        pltpu.make_async_copy(source, target, sems.at[i])
        for i, (source, target) in enumerate(copies)
    ]
    for copy in started:
        copy.start()
    for copy in started:
        copy.wait()
    for end, out in enumerate((head, tail)):
        out[0:2] = cells[end]
        skip = 0 if end == 0 else 16 - width
        for k in range(count):
            out[2 + k] = deltas[end, k].astype(F32)[skip : skip + width]
            out[2 + count + k] = absorbs[end, k].astype(F32)[skip : skip + width]


def turn_kernel(height, count, width, index_ref, loss_ref, out, turned):
    length = index_ref.shape[2]
    side = 2 * LANES
    diagonal = lax.broadcasted_iota(jnp.int32, (side, side), 0) == lax.broadcasted_iota(
        jnp.int32, (side, side), 1
    )
    identity = jnp.where(diagonal, 1.0, 0.0).astype(BF16)
    margin = jnp.zeros((width, height), F32)
    for which, source in enumerate((index_ref, loss_ref)):
        for k in range(count):
            line = which * count + k
            turned[line, 0:width, :] = margin
            turned[line, width + length :, :] = margin
            for start in range(0, length, side):
                turned[line, width + start : width + start + side, :] = lax.dot_general(
                    identity,
                    source[k, :, start : start + side],
                    (((1,), (1,)), ((), ())),
                    preferred_element_type=F32,
                )
    for k in range(out.shape[0]):
        for line in range(2 * count):
            out[k, line] = turned[line, k * height : k * height + height + 2 * width, :].astype(BF16)


def put_coded(out, first, natural, rows, scale):
    start, stop = rows
    for i in range(natural.shape[0]):
        out[first : first + stop - start, i * LANES : (i + 1) * LANES] = encode(
            natural[i, start:stop, :], scale
        )


def put_scale(out, first, scale):
    out[first : first + SCALE_ROWS, :] = jnp.broadcast_to(
        scale, (SCALE_ROWS, out.shape[1])
    ).astype(BF16)


def inner_kernel(
    height, count, width, field, index_ref, loss_ref, out,
    buf0, buf1, buf2, phase, loss, keep, natural,
):
    bufs = (buf0, buf1, buf2)
    for part in range(2):
        for row in range(0, height, 16):
            by_blocks(natural.at[part], row, field[part, row : row + 16, :])
        spread_rows(natural.at[part], buf0.at[part], 1)
    wrap(buf0, height // 8)

    def load_coefficients(k):
        for which, (source, scale, target) in enumerate(
            ((index_ref, scaled_phase, phase), (loss_ref, scaled_loss, loss))
        ):
            for row in range(0, height, 16):
                by_blocks(natural.at[which], row, scale(source[k, row : row + 16, :]))
            spread_rows(natural.at[which], target, 0)

    apply_slices(count, width, None, load_coefficients, bufs, phase, loss, keep)
    for part in range(2):
        gather_rows(buf0.at[part], 1, natural.at[part])
    rows = (width, height - width)
    inner = height - 2 * width
    scale = scale_of([natural[part, :, width : height - width, :] for part in range(2)])
    for part in range(2):
        put_coded(out, part * inner, natural.at[part], rows, scale)
    put_scale(out, 2 * inner, scale)


def outer_kernel(
    height, count, width, edge_ref, field, above, below, index_ref, loss_ref, out,
    buf0, buf1, buf2, phase, loss, keep, natural,
):
    bufs = (buf0, buf1, buf2)
    own = 2 * width
    tall = 6 * width

    def place(target, line, ends):
        by_blocks(target, 0, above[line].astype(F32))
        by_blocks(target, width, ends[0].astype(F32))
        by_blocks(target, width + own, ends[1].astype(F32))
        by_blocks(target, width + 2 * own, below[line].astype(F32))

    for part in range(2):
        place(natural.at[part], part, (field[part, 0:own, :], field[part, height - own :, :]))
        spread_rows(natural.at[part], buf0.at[part], 1)
    wrap(buf0, tall // 8)

    def load_coefficients(k):
        for which, (source, scale, target) in enumerate(
            ((index_ref, scaled_phase, phase), (loss_ref, scaled_loss, loss))
        ):
            line = 2 + which * count + k
            place(natural.at[which], line, (source[k, 0:own, :], source[k, height - own :, :]))
            for i in range(natural.shape[1]):
                natural[which, i] = scale(natural[which, i])
            spread_rows(natural.at[which], target, 0)

    inside = (edge_ref[0], edge_ref[1])
    apply_slices(count, width, inside, load_coefficients, bufs, phase, loss, keep)
    for part in range(2):
        gather_rows(buf0.at[part], 1, natural.at[part])
    ends = ((width, 2 * width), (4 * width, 5 * width))
    scale = scale_of([natural[part, :, s:e, :] for part in range(2) for s, e in ends])
    for part in range(2):
        for i in range(natural.shape[1]):
            both = jnp.concatenate([natural[part, i, s:e, :] for s, e in ends], axis=0)
            out[part * own : (part + 1) * own, i * LANES : (i + 1) * LANES] = encode(both, scale)
    put_scale(out, 2 * own, scale)


def rows_kernel(height, width, inner_ref, outer_ref, tables, out, field, spectrum):
    length = inner_ref.shape[1]
    inner = height - 2 * width

    def scale_in(ref, row):
        return ref[row : row + SCALE_ROWS, :].astype(F32)[0:1]

    inner_scale = scale_in(inner_ref, 2 * inner)
    outer_scale = scale_in(outer_ref, 4 * width)
    for part in range(2):
        start = part * height
        ends = decode(outer_ref[2 * part * width : 2 * (part + 1) * width, :], outer_scale)
        field[start : start + width, :] = ends[:width]
        field[start + height - width : start + height, :] = ends[width:]
        for row in range(0, inner, 16):
            field[start + width + row : start + width + row + 16, :] = decode(
                inner_ref[part * inner + row : part * inner + row + 16, :], inner_scale
            )
    halves = gap_transposed(tables, field[...], height)
    half = length // 2
    spectrum[0:width, :] = jnp.zeros((width, 2 * height), F32)
    spectrum[width + length :, :] = jnp.zeros((width, 2 * height), F32)
    for which, (real, imag) in enumerate(halves):
        start = width + which * half
        spectrum[start : start + half, :height] = real
        spectrum[start : start + half, height:] = imag
    scale = scale_of([part for pair in halves for part in pair])
    tall = height + 2 * width
    for k in range(out.shape[0]):
        out[k, 0:tall, :] = encode(spectrum[k * height : k * height + tall, :], scale)
        put_scale(out.at[k], tall, scale)


def second_kernel(
    height, count, width, edge_ref, blocks, specimen, tables, out,
    buf0, buf1, buf2, phase, loss, keep, natural,
):
    bufs = (buf0, buf1, buf2)
    tall = height + 2 * width
    length = out.shape[0] * height
    half = length // 2
    for which, halves in enumerate(gap_from_blocks(tables, blocks, tall)):
        for part in range(2):
            by_blocks(natural.at[part, pl.ds(which * half // LANES, half // LANES)], 0, halves[part])
    inside = (edge_ref[0], edge_ref[1])
    for part in range(2):
        for i in range(natural.shape[1]):
            for end, rows in enumerate((slice(0, width), slice(tall - width, tall))):
                line = natural[part, i, rows, :]
                natural[part, i, rows, :] = jnp.where(inside[end] > 0, line, 0.0)
        spread_rows(natural.at[part], buf0.at[part], 1)
    wrap(buf0, tall // 8)

    def load_coefficients(k):
        for which, (scale, target) in enumerate(((scaled_phase, phase), (scaled_loss, loss))):
            for i in range(specimen.shape[0]):
                for row in range(0, tall, 16):
                    natural[which, i, row : row + 16, :] = scale(
                        specimen[i, which * count + k, row : row + 16, :]
                    )
            spread_rows(natural.at[which], target, 0)

    apply_slices(count, width, inside, load_coefficients, bufs, phase, loss, keep)
    for part in range(2):
        gather_rows(buf0.at[part], 1, natural.at[part])
    halves = gap_transposed(tables, joined(natural, width, height), height)
    scale = scale_of([part for pair in halves for part in pair])
    rows_of_half = out.shape[0] // 2
    for which, (real, imag) in enumerate(halves):
        for k in range(rows_of_half):
            rows = slice(k * height, (k + 1) * height)
            target = which * rows_of_half + k
            out[target, 0:height, :height] = encode(real[rows], scale)
            out[target, 0:height, height:] = encode(imag[rows], scale)
            out[target, height:, :] = jnp.broadcast_to(scale, (SCALE_ROWS, 2 * height)).astype(BF16)


def third_kernel(height, blocks, tables, out):
    half = out.shape[2] // 2
    for which, (real, imag) in enumerate(gap_from_blocks(tables, blocks, height)):
        out[0, :, which * half : (which + 1) * half] = real
        out[1, :, which * half : (which + 1) * half] = imag


VMEM = pl.BlockSpec(memory_space=pltpu.VMEM)
SMEM = pl.BlockSpec(memory_space=pltpu.SMEM)
HBM = pl.BlockSpec(memory_space=pltpu.HBM)


def call(kernel, in_specs, out_shape, scratch, name, flops, moved, outs=1):
    return pl.pallas_call(
        kernel,
        in_specs=in_specs,
        out_specs=VMEM if outs == 1 else (VMEM,) * outs,
        out_shape=out_shape,
        scratch_shapes=scratch,
        compiler_params=pltpu.CompilerParams(vmem_limit_bytes=VMEM_BYTES),
        cost_estimate=pl.CostEstimate(flops=flops, bytes_accessed=moved, transcendentals=0),
        name=name,
    )


def in_lane_blocks(pieces):
    sources, rows, both = pieces.shape
    own = both // 2
    if own == LANES:
        return pieces
    joined = pieces.reshape(sources, rows, 2, own).transpose(1, 2, 0, 3)
    joined = joined.reshape(rows, 2, sources * own // LANES, LANES).transpose(2, 0, 1, 3)
    return joined.reshape(sources * own // LANES, rows, 2 * LANES)


def to_others(pieces):
    return lax.all_to_all(pieces, "rows", split_axis=0, concat_axis=0, tiled=True)


def local(in_flight, phase_index, absorption):
    field = in_flight[0]
    count, height, length = phase_index.shape
    slabs = lax.axis_size("rows")
    groups = lax.axis_size("depth")
    width = count * TAYLOR
    tall = height + 2 * width
    place = lax.axis_index("rows")
    edge = jnp.stack([(place > 0), (place < slabs - 1)]).astype(jnp.int32)
    tables = jnp.asarray(gap_tables(length))

    lane_blocks = length // LANES

    def working(rows):
        buffer = pltpu.VMEM((2, lane_blocks, rows + 16, LANES), F32)
        coefficient = pltpu.VMEM((lane_blocks, rows, LANES), F32)
        return [buffer] * 3 + [coefficient] * 2 + [
            pltpu.VMEM((rows, LANES), F32),
            pltpu.VMEM((2, lane_blocks, rows, LANES), F32),
        ]

    def slice_cost(rows):
        cells = count * TAYLOR * rows * length
        return 40 * cells, 32 * cells

    gap_flops = 24 * height * length * length // 2
    to_next = [(g, (g + 1) % groups) for g in range(groups)]

    turned = call(
        functools.partial(turn_kernel, height, count, width),
        [VMEM] * 2,
        jax.ShapeDtypeStruct((slabs, 2 * count, tall, height), BF16),
        [pltpu.VMEM((2 * count, length + 2 * width, height), F32)],
        "specimen_columns",
        0,
        0,
    )(phase_index, absorption)
    turned, field = lax.optimization_barrier((turned, field))
    specimen = to_others(turned)

    inner = call(
        functools.partial(inner_kernel, height, count, width),
        [VMEM] * 3,
        jax.ShapeDtypeStruct((2 * (height - 2 * width) + SCALE_ROWS, length), BF16),
        working(height),
        "slices_inner_rows",
        *slice_cost(height),
    )(field, phase_index, absorption)
    inner, late_field = lax.optimization_barrier((inner, field))
    inner = lax.ppermute(inner, "depth", to_next)

    line_shape = jax.ShapeDtypeStruct((2 + 2 * count, width, length), F32)
    head, tail = call(
        functools.partial(lines_kernel, height, count, width),
        [HBM] * 3,
        (line_shape, line_shape),
        [
            pltpu.VMEM((2, 2, width, length), F32),
            pltpu.VMEM((2, count, 16, length), BF16),
            pltpu.VMEM((2, count, 16, length), BF16),
            pltpu.SemaphoreType.DMA((6,)),
        ],
        "edge_lines",
        0,
        0,
        2,
    )(late_field, phase_index, absorption)
    down = [(i, i + 1) for i in range(slabs - 1)]
    up = [(i + 1, i) for i in range(slabs - 1)]
    above = lax.ppermute(tail, "rows", down)
    below = lax.ppermute(head, "rows", up)
    outer = call(
        functools.partial(outer_kernel, height, count, width),
        [SMEM] + [VMEM] * 5,
        jax.ShapeDtypeStruct((4 * width + SCALE_ROWS, length), BF16),
        working(6 * width),
        "slices_outer_rows",
        0,
        0,
    )(edge, late_field, above, below, phase_index, absorption)

    outer = lax.ppermute(outer, "depth", to_next)
    if height != LANES:
        specimen = specimen.transpose(1, 2, 0, 3).reshape(2 * count, tall, -1, LANES)
        specimen = specimen.transpose(2, 0, 1, 3)

    pieces = call(
        functools.partial(rows_kernel, height, width),
        [VMEM] * 3,
        jax.ShapeDtypeStruct((slabs, tall + SCALE_ROWS, 2 * height), BF16),
        [
            pltpu.VMEM((2 * height, length), F32),
            pltpu.VMEM((length + 2 * width, 2 * height), F32),
        ],
        "gap_along_rows",
        gap_flops,
        8 * 1024 * 1024,
    )(inner, outer, tables)
    pieces, specimen = lax.optimization_barrier((pieces, specimen))
    blocks = in_lane_blocks(to_others(pieces))

    pieces = call(
        functools.partial(second_kernel, height, count, width),
        [SMEM] + [VMEM] * 3,
        jax.ShapeDtypeStruct((slabs, height + SCALE_ROWS, 2 * height), BF16),
        working(tall),
        "gap_slices_gap_columns",
        *slice_cost(tall),
    )(edge, blocks, specimen, tables)

    blocks = in_lane_blocks(to_others(pieces))

    field = call(
        functools.partial(third_kernel, height),
        [VMEM] * 2,
        jax.ShapeDtypeStruct((2, height, length), F32),
        [],
        "gap_rows",
        gap_flops,
        6 * 1024 * 1024,
    )(blocks, tables)
    return field[None]


def solution(mesh):
    placed = (P("depth", None, "rows", None), P("depth", "rows", None), P("depth", "rows", None))
    return jax.shard_map(
        local, mesh=mesh, in_specs=placed, out_specs=P("depth", None, "rows", None), check_vma=False
    )
```

```python
import functools
import math

import jax
import jax.numpy as jnp
import ml_dtypes
import numpy as np
from jax import lax
from jax.experimental import pallas as pl
from jax.experimental.pallas import tpu as pltpu
from jax.sharding import PartitionSpec as P

TAYLOR = 4
LATERAL = 0.22
CONTRAST = 0.2
LANES = 128
VMEM_BYTES = 24 * 1024 * 1024
ALL_VMEM_BYTES = 60 * 1024 * 1024
F32 = jnp.float32
BF16 = jnp.bfloat16


def circulant_split(column):
    length = column.shape[0]
    half = length // 2
    lag = np.arange(half)[:, None] - np.arange(half)[None, :]
    near, far = column[lag % length], column[(lag + half) % length]
    return (near + far) / 2, (near - far) / 2


def interleave(length):
    return np.arange(length).reshape(-1, LANES, 2).transpose(0, 2, 1).reshape(-1)


def gap_tables(length, interleaved):
    frequency = np.arange(length)
    frequency = np.where(frequency < length // 2, frequency, frequency - length)
    response = np.exp(-1j * math.pi * (frequency * frequency % (8 * length)) / (4 * length))
    even, odd = circulant_split(np.fft.ifft(response))
    parts = []
    for blocks in (circulant_split(even[:, 0]), (odd,)):
        table = np.stack([t for block in blocks for t in (block.real, block.imag)])
        if interleaved:
            table = table[:, :, interleave(table.shape[2])]
        table = table.astype(np.float32)
        high = table.astype(ml_dtypes.bfloat16)
        low = (table - high.astype(np.float32)).astype(ml_dtypes.bfloat16)
        parts.append(jnp.asarray(np.stack([high, low])))
    return parts


FLOOR = 255.0
SPAN = 250.0
STEEP = SPAN / math.log2(1.0 + FLOOR)
SCALE_ROWS = 16


def scale_of(arrays):
    largest = functools.reduce(jnp.maximum, [jnp.max(jnp.abs(array)) for array in arrays])
    return jnp.maximum(largest * (1.0 + 2.0**-7), 1e-30).astype(BF16).astype(F32)


def encode(values, scale):
    level = jnp.log2(1.0 + jnp.abs(values) * (FLOOR / scale))
    code = jnp.exp2(level * STEEP - SPAN / 2)
    return jnp.where(values < 0, -code, code).astype(BF16)


def decode(codes, scale):
    codes = codes.astype(F32)
    level = (jnp.log2(jnp.abs(codes)) + SPAN / 2) * (1.0 / STEEP)
    values = (jnp.exp2(level) - 1.0) * (scale * (1.0 / FLOOR))
    return jnp.where(codes < 0, -values, values)


def decode_block(blocks_ref, i, lane, rows):
    lanes = slice(lane, lane + LANES)
    scale = blocks_ref[i, rows : rows + SCALE_ROWS, lanes].astype(F32)[0:1]
    return decode(blocks_ref[i, 0:rows, lanes], scale)


def split(values):
    high = values.astype(BF16)
    return high, (values - high.astype(F32)).astype(BF16)


def product(tables, which, operand, transposed):
    high, low = operand

    def dot(part, data):
        table = tables[part, which]
        if transposed:
            return lax.dot_general(table, data, (((1,), (1,)), ((), ())), preferred_element_type=F32)
        return lax.dot_general(data, table, (((1,), (0,)), ((), ())), preferred_element_type=F32)

    return dot(0, high) + (dot(1, high) + dot(0, low))


def half_gap(tables, first, stacked, rows, transposed):
    operand = split(stacked)
    by_re = product(tables, first, operand, transposed)
    by_im = product(tables, first + 1, operand, transposed)
    if transposed:
        return (by_re[:, :rows] - by_im[:, rows:], by_re[:, rows:] + by_im[:, :rows])
    return (by_re[:rows] - by_im[rows:], by_re[rows:] + by_im[:rows])


def gap_of_parts(tables, even, odd, rows, transposed):
    small, large = tables
    quarter = even.shape[1] // 2
    left, right = even[:, :quarter], even[:, quarter:]
    sums = half_gap(small, 0, left + right, rows, transposed)
    differences = half_gap(small, 2, left - right, rows, transposed)
    axis = 0 if transposed else 1
    even = [
        jnp.concatenate([x + y, x - y], axis=axis) for x, y in zip(sums, differences, strict=True)
    ]
    odd = half_gap(large, 0, odd, rows, transposed)
    return [(even[0] + odd[0], even[1] + odd[1]), (even[0] - odd[0], even[1] - odd[1])]


def gap_transposed(tables, field, rows):
    half = field.shape[1] // 2
    left, right = field[:, :half], field[:, half:]
    return gap_of_parts(tables, left + right, left - right, rows, True)


def gap_from_blocks(tables, blocks_ref, rows):
    count = blocks_ref.shape[0] // 2

    parts = [
        [decode_block(blocks_ref, i, lane, rows) for i in range(2 * count)] for lane in (0, LANES)
    ]

    def folded(sign):
        return jnp.concatenate(
            [
                jnp.concatenate([part[i] + sign * part[i + count] for i in range(count)], axis=1)
                for part in parts
            ],
            axis=0,
        )

    return gap_of_parts(tables, folded(1.0), folded(-1.0), rows, False)


def shifted(row):
    lane = lax.broadcasted_iota(jnp.int32, row[0].shape, 1)
    count = len(row)
    moved_right = [pltpu.roll(row[i], 1, 1) for i in range(1, count, 2)]
    moved_left = [pltpu.roll(row[i], LANES - 1, 1) for i in range(0, count, 2)]
    before, after = [], []
    for i in range(count // 2):
        outside = moved_right[i - 1] if i else 0.0
        before += [jnp.where(lane == 0, outside, moved_right[i]), row[2 * i]]
        outside = moved_left[i + 1] if 2 * i + 2 < count else 0.0
        after += [row[2 * i + 1], jnp.where(lane == LANES - 1, outside, moved_left[i])]
    return before, after


def spread_rows(natural, target, first):
    blocks, tall, _ = natural.shape
    steps = tall // 8
    for i in range(blocks):
        for k in range(steps):
            target[i, 8 * (k + first) : 8 * (k + first) + 8, :] = natural.at[i][
                pl.ds(k, 8, stride=steps), :
            ]


def gather_rows(source, first, natural):
    blocks, tall, _ = natural.shape
    steps = tall // 8
    for i in range(blocks):
        for k in range(steps):
            natural.at[i][pl.ds(k, 8, stride=steps), :] = source[
                i, 8 * (k + first) : 8 * (k + first) + 8, :
            ]


def wrap(buf, steps):
    for part in range(2):
        for i in range(buf.shape[1]):
            last = buf[part, i, 8 * steps : 8 * steps + 8, :]
            buf[part, i, 0:8, :] = pltpu.roll(last, 1, 0)
            initial = buf[part, i, 8:16, :]
            buf[part, i, 8 * steps + 8 : 8 * steps + 16, :] = pltpu.roll(initial, 7, 0)


def apply_slices(count, width, inside, bufs, phase, loss, keep):
    _, blocks, tall, _ = phase.shape
    steps = tall // 8
    sublane = lax.broadcasted_iota(jnp.int32, (8, LANES), 0)
    for k in range(steps if inside else 0):
        row = sublane * steps + k
        top = jnp.logical_and(row < width, inside[0] == 0)
        bottom = jnp.logical_and(row >= tall - width, inside[1] == 0)
        keep[8 * k : 8 * k + 8, :] = jnp.where(jnp.logical_or(top, bottom), 0.0, 1.0)
    base = bufs[0]

    def step(slice_index, source, target, weight):
        def body(k):
            def rows(ref, at, *lead):
                start = (k + at) * 8
                return [ref[lead + (i, pl.ds(start, 8), slice(None))] for i in range(blocks)]

            factor = keep[pl.ds(k * 8, 8), :] * weight if inside else weight
            phases = rows(phase, 0, slice_index)
            losses = rows(loss, 0, slice_index)
            here, total = [], []
            for part in range(2):
                cells = rows(source, 1, part)
                above, below = rows(source, 0, part), rows(source, 2, part)
                before, after = shifted(cells)
                here.append(cells)
                total.append(
                    [
                        (above[i] + below[i]) + (before[i] + after[i]) + phases[i] * cells[i]
                        for i in range(blocks)
                    ]
                )
            start = pl.ds((k + 1) * 8, 8)
            for i in range(blocks):
                target[0, i, start, :] = base[0, i, start, :] - factor * (
                    total[1][i] + losses[i] * here[0][i]
                )
                target[1, i, start, :] = base[1, i, start, :] + factor * (
                    total[0][i] - losses[i] * here[1][i]
                )

        for k in range(steps):
            body(k)
        wrap(target, steps)

    def one_slice(slice_index, carry):
        source = bufs[0]
        for degree in range(TAYLOR, 0, -1):
            target = bufs[0] if degree == 1 else bufs[1 + degree % 2]
            step(slice_index, source, target, LATERAL / degree)
            source = target
        return carry

    lax.fori_loop(0, count, one_slice, 0)


def scaled_phase(values):
    return values.astype(F32) * (CONTRAST / LATERAL) - 4.0


def scaled_loss(values):
    return values.astype(F32) * (CONTRAST / LATERAL)


def by_blocks(target, start, values):
    rows = values.shape[0]
    for i in range(values.shape[1] // LANES):
        target[i, start : start + rows, :] = values[:, i * LANES : (i + 1) * LANES]


def interleaving():
    side = 2 * LANES
    line = lax.broadcasted_iota(jnp.int32, (side, side), 0)
    place = lax.broadcasted_iota(jnp.int32, (side, side), 1)
    chosen = line == 2 * (place % LANES) + place // LANES
    return jnp.where(chosen, 1.0, 0.0).astype(BF16)


def interleaved(field, specimen):
    order = interleaving()
    side = 2 * LANES
    rows = field.shape[0] if field is not None else 0
    for first in range(0, specimen.shape[1], side):
        parts = [specimen[:, first : first + side]]
        if rows:
            rest = field[:, first : first + side]
            for _ in range(3):
                part = rest.astype(BF16)
                parts.append(part)
                rest = rest - part.astype(F32)
        lines = lax.dot_general(
            jnp.concatenate(parts, axis=0) if rows else parts[0],
            order,
            (((1,), (0,)), ((), ())),
            preferred_element_type=F32,
        )
        own = specimen.shape[0]
        cells = None
        if rows:
            high, mid, low = (lines[own + i * rows : own + (i + 1) * rows] for i in range(3))
            cells = high + (mid + low)
        yield first // LANES, cells, lines[:own]


def spread_interleaved(field, specimen, count, natural, buf, phase, loss):
    rows = specimen.shape[0] // (2 * count)
    for block, cells, lines in interleaved(field, specimen):
        blocks = pl.ds(block, 2)
        for part in range(2):
            by_blocks(natural.at[part, blocks], 0, cells[part * rows : (part + 1) * rows])
        for k in range(2 * count):
            scale = scaled_phase if k < count else scaled_loss
            by_blocks(natural.at[2 + k, blocks], 0, scale(lines[k * rows : (k + 1) * rows]))
    for part in range(2):
        spread_rows(natural.at[part], buf.at[part], 1)
    wrap(buf, rows // 8)
    for k in range(count):
        spread_rows(natural.at[2 + k], phase.at[k], 0)
        spread_rows(natural.at[2 + count + k], loss.at[k], 0)


def joined(natural, start, rows):
    return jnp.concatenate(
        [
            jnp.concatenate(
                [natural[part, i, start : start + rows, :] for i in range(natural.shape[1])], axis=1
            )
            for part in range(2)
        ],
        axis=0,
    )


def lines_kernel(
    height, count, width, field, index_ref, loss_ref, head, tail, cells, deltas, absorbs, sems
):
    copies = []
    for end, start in enumerate((0, height - width)):
        copies.append((field.at[:, pl.ds(start, width)], cells.at[end]))
    for end, start in enumerate((0, height - 16)):
        copies.append((index_ref.at[:, pl.ds(start, 16)], deltas.at[end]))
        copies.append((loss_ref.at[:, pl.ds(start, 16)], absorbs.at[end]))
    started = [
        pltpu.make_async_copy(source, target, sems.at[i])
        for i, (source, target) in enumerate(copies)
    ]
    for copy in started:
        copy.start()
    for copy in started:
        copy.wait()
    for end, out in enumerate((head, tail)):
        out[0:2] = cells[end]
        skip = 0 if end == 0 else 16 - width
        for k in range(count):
            out[2 + k] = deltas[end, k].astype(F32)[skip : skip + width]
            out[2 + count + k] = absorbs[end, k].astype(F32)[skip : skip + width]


def turn_kernel(height, count, width, index_ref, loss_ref, out, turned):
    length = index_ref.shape[2]
    side = 2 * LANES
    diagonal = lax.broadcasted_iota(jnp.int32, (side, side), 0) == lax.broadcasted_iota(
        jnp.int32, (side, side), 1
    )
    identity = jnp.where(diagonal, 1.0, 0.0).astype(BF16)
    margin = jnp.zeros((width, height), F32)
    for which, source in enumerate((index_ref, loss_ref)):
        for k in range(count):
            line = which * count + k
            turned[line, 0:width, :] = margin
            turned[line, width + length :, :] = margin
            for start in range(0, length, side):
                turned[line, width + start : width + start + side, :] = lax.dot_general(
                    identity,
                    source[k, :, start : start + side],
                    (((1,), (1,)), ((), ())),
                    preferred_element_type=F32,
                )
    for k in range(out.shape[0]):
        for line in range(2 * count):
            out[k, line] = turned[line, k * height : k * height + height + 2 * width, :].astype(BF16)


def put_coded(out, first, natural, rows, scale):
    start, stop = rows
    for i in range(natural.shape[0]):
        out[first : first + stop - start, i * LANES : (i + 1) * LANES] = encode(
            natural[i, start:stop, :], scale
        )


def put_scale(out, first, scale):
    out[first : first + SCALE_ROWS, :] = jnp.broadcast_to(
        scale, (SCALE_ROWS, out.shape[1])
    ).astype(BF16)


def inner_kernel(
    height, count, width, field, index_ref, loss_ref, out,
    buf0, buf1, buf2, phase, loss, keep, natural,
):
    bufs = (buf0, buf1, buf2)
    length = field.shape[2]
    specimen = [ref[...].reshape(count * height, length) for ref in (index_ref, loss_ref)]
    spread_interleaved(
        field[...].reshape(2 * height, length),
        jnp.concatenate(specimen, axis=0),
        count, natural, buf0, phase, loss,
    )
    apply_slices(count, width, None, bufs, phase, loss, keep)
    for part in range(2):
        gather_rows(buf0.at[part], 1, natural.at[part])
    rows = (width, height - width)
    inner = height - 2 * width
    scale = scale_of([natural[part, :, width : height - width, :] for part in range(2)])
    for part in range(2):
        put_coded(out, part * inner, natural.at[part], rows, scale)
    put_scale(out, 2 * inner, scale)


def outer_kernel(
    height, count, width, edge_ref, field, above, below, index_ref, loss_ref, ready, out,
    buf0, buf1, buf2, phase, loss, keep, natural,
):
    del ready
    bufs = (buf0, buf1, buf2)
    own = 2 * width

    def around(line, source, k):
        lines = [above[line], source[k, 0:own, :], source[k, height - own :, :], below[line]]
        return [part.astype(F32) for part in lines]

    cells = around(0, field, 0) + around(1, field, 1)
    specimen = []
    for which, source in enumerate((index_ref, loss_ref)):
        for k in range(count):
            specimen += around(2 + which * count + k, source, k)
    spread_interleaved(
        jnp.concatenate(cells, axis=0),
        jnp.concatenate(specimen, axis=0).astype(BF16),
        count, natural, buf0, phase, loss,
    )
    inside = (edge_ref[0], edge_ref[1])
    apply_slices(count, width, inside, bufs, phase, loss, keep)
    for part in range(2):
        gather_rows(buf0.at[part], 1, natural.at[part])
    ends = ((width, 2 * width), (4 * width, 5 * width))
    scale = scale_of([natural[part, :, s:e, :] for part in range(2) for s, e in ends])
    for part in range(2):
        for i in range(natural.shape[1]):
            both = jnp.concatenate([natural[part, i, s:e, :] for s, e in ends], axis=0)
            out[part * own : (part + 1) * own, i * LANES : (i + 1) * LANES] = encode(both, scale)
    put_scale(out, 2 * own, scale)


def rows_kernel(
    height, width, inner_ref, outer_ref, small, large, out, field, spectrum
):
    tables = (small, large)
    length = inner_ref.shape[1]
    inner = height - 2 * width

    def scale_in(ref, row):
        return ref[row : row + SCALE_ROWS, :].astype(F32)[0:1]

    inner_scale = scale_in(inner_ref, 2 * inner)
    outer_scale = scale_in(outer_ref, 4 * width)
    for part in range(2):
        start = part * height
        ends = decode(outer_ref[2 * part * width : 2 * (part + 1) * width, :], outer_scale)
        field[start : start + width, :] = ends[:width]
        field[start + height - width : start + height, :] = ends[width:]
        for row in range(0, inner, 16):
            field[start + width + row : start + width + row + 16, :] = decode(
                inner_ref[part * inner + row : part * inner + row + 16, :], inner_scale
            )
    halves = gap_transposed(tables, field[...], height)
    half = length // 2
    spectrum[0:width, :] = jnp.zeros((width, 2 * height), F32)
    spectrum[width + length :, :] = jnp.zeros((width, 2 * height), F32)
    for which, (real, imag) in enumerate(halves):
        start = width + which * half
        spectrum[start : start + half, :height] = real
        spectrum[start : start + half, height:] = imag
    scale = scale_of([part for pair in halves for part in pair])
    tall = height + 2 * width
    for k in range(out.shape[0]):
        out[k, 0:tall, :] = encode(spectrum[k * height : k * height + tall, :], scale)
        put_scale(out.at[k], tall, scale)


def coefficients_kernel(count, specimen, out, natural):
    tall = natural.shape[2]
    lines = jnp.concatenate(
        [specimen[i].reshape(2 * count * tall, LANES) for i in range(specimen.shape[0])], axis=1
    )
    for block, _, cells in interleaved(None, lines):
        for k in range(2 * count):
            scale = scaled_phase if k < count else scaled_loss
            part = scale(cells[k * tall : (k + 1) * tall])
            by_blocks(natural.at[k, pl.ds(block, 2)], 0, part)
    for k in range(2 * count):
        spread_rows(natural.at[k], out.at[k // count, k % count], 0)


def second_kernel(
    height, count, width, edge_ref, blocks, coefficients, small, large, out,
    buf0, buf1, buf2, keep, natural,
):
    tables = (small, large)
    bufs = (buf0, buf1, buf2)
    tall = height + 2 * width
    length = out.shape[0] * height
    half = length // 2
    for which, halves in enumerate(gap_from_blocks(tables, blocks, tall)):
        for part in range(2):
            by_blocks(natural.at[part, pl.ds(which * half // LANES, half // LANES)], 0, halves[part])
    inside = (edge_ref[0], edge_ref[1])
    for part in range(2):
        for i in range(natural.shape[1]):
            for end, rows in enumerate((slice(0, width), slice(tall - width, tall))):
                line = natural[part, i, rows, :]
                natural[part, i, rows, :] = jnp.where(inside[end] > 0, line, 0.0)
        spread_rows(natural.at[part], buf0.at[part], 1)
    wrap(buf0, tall // 8)
    apply_slices(count, width, inside, bufs, coefficients.at[0], coefficients.at[1], keep)
    for part in range(2):
        gather_rows(buf0.at[part], 1, natural.at[part])
    halves = gap_transposed(tables, joined(natural, width, height), height)
    scale = scale_of([part for pair in halves for part in pair])
    rows_of_half = out.shape[0] // 2
    for which, (real, imag) in enumerate(halves):
        for k in range(rows_of_half):
            rows = slice(k * height, (k + 1) * height)
            target = which * rows_of_half + k
            out[target, 0:height, :height] = encode(real[rows], scale)
            out[target, 0:height, height:] = encode(imag[rows], scale)
            put_scale(out.at[target], height, scale)


def third_kernel(height, blocks, small, large, out):
    half = out.shape[2] // 2
    halves = gap_from_blocks((small, large), blocks, height)
    for which, (real, imag) in enumerate(halves):
        out[0, :, which * half : (which + 1) * half] = real
        out[1, :, which * half : (which + 1) * half] = imag


VMEM = pl.BlockSpec(memory_space=pltpu.VMEM)
SMEM = pl.BlockSpec(memory_space=pltpu.SMEM)
ANY = pl.BlockSpec(memory_space=pl.ANY)


def call(kernel, in_specs, out_shape, scratch, name, flops, moved, outs=1, room=VMEM_BYTES):
    return pl.pallas_call(
        kernel,
        in_specs=in_specs,
        out_specs=VMEM if outs == 1 else (VMEM,) * outs,
        out_shape=out_shape,
        scratch_shapes=scratch,
        compiler_params=pltpu.CompilerParams(vmem_limit_bytes=room),
        cost_estimate=pl.CostEstimate(flops=flops, bytes_accessed=moved, transcendentals=0),
        name=name,
    )


def in_lane_blocks(pieces):
    sources, rows, both = pieces.shape
    own = both // 2
    if own == LANES:
        return pieces
    joined = pieces.reshape(sources, rows, 2, own).transpose(1, 2, 0, 3)
    joined = joined.reshape(rows, 2, sources * own // LANES, LANES).transpose(2, 0, 1, 3)
    return joined.reshape(sources * own // LANES, rows, 2 * LANES)


def to_others(pieces):
    return lax.all_to_all(pieces, "rows", split_axis=0, concat_axis=0, tiled=True)


def local(in_flight, phase_index, absorption):
    field = in_flight[0]
    count, height, length = phase_index.shape
    slabs = lax.axis_size("rows")
    groups = lax.axis_size("depth")
    width = count * TAYLOR
    tall = height + 2 * width
    place = lax.axis_index("rows")
    edge = jnp.stack([(place > 0), (place < slabs - 1)]).astype(jnp.int32)
    tables = gap_tables(length, False)
    tables_interleaved = gap_tables(length, True)

    lane_blocks = length // LANES

    def working(rows, specimen):
        buffer = pltpu.VMEM((2, lane_blocks, rows + 16, LANES), F32)
        coefficient = pltpu.VMEM((count, lane_blocks, rows, LANES), F32)
        arrays = 2 + 2 * count if specimen else 2
        return [buffer] * 3 + [coefficient] * (2 if specimen else 0) + [
            pltpu.VMEM((rows, LANES), F32),
            pltpu.VMEM((arrays, lane_blocks, rows, LANES), F32),
        ]

    def slice_cost(rows):
        cells = count * TAYLOR * rows * length
        return 40 * cells, 32 * cells

    gap_flops = 24 * height * length * length // 2
    to_next = [(g, (g + 1) % groups) for g in range(groups)]

    turned = call(
        functools.partial(turn_kernel, height, count, width),
        [VMEM] * 2,
        jax.ShapeDtypeStruct((slabs, 2 * count, tall, height), BF16),
        [pltpu.VMEM((2 * count, length + 2 * width, height), F32)],
        "specimen_columns",
        0,
        0,
        room=ALL_VMEM_BYTES,
    )(phase_index, absorption)
    turned, field = lax.optimization_barrier((turned, field))
    specimen = to_others(turned)

    inner = call(
        functools.partial(inner_kernel, height, count, width),
        [VMEM] * 3,
        jax.ShapeDtypeStruct((2 * (height - 2 * width) + SCALE_ROWS, length), BF16),
        working(height, True),
        "slices_inner_rows",
        *slice_cost(height),
    )(field, phase_index, absorption)
    inner, late_field = lax.optimization_barrier((inner, field))
    inner = lax.ppermute(inner, "depth", to_next)

    line_shape = jax.ShapeDtypeStruct((2 + 2 * count, width, length), F32)
    head, tail = call(
        functools.partial(lines_kernel, height, count, width),
        [ANY] * 3,
        (line_shape, line_shape),
        [
            pltpu.VMEM((2, 2, width, length), F32),
            pltpu.VMEM((2, count, 16, length), BF16),
            pltpu.VMEM((2, count, 16, length), BF16),
            pltpu.SemaphoreType.DMA((6,)),
        ],
        "edge_lines",
        0,
        0,
        2,
    )(late_field, phase_index, absorption)
    down = [(i, i + 1) for i in range(slabs - 1)]
    up = [(i + 1, i) for i in range(slabs - 1)]
    above = lax.ppermute(tail, "rows", down)
    below = lax.ppermute(head, "rows", up)
    if height != LANES:
        specimen = specimen.transpose(1, 2, 0, 3).reshape(2 * count, tall, -1, LANES)
        specimen = specimen.transpose(2, 0, 1, 3)
    coefficients = call(
        functools.partial(coefficients_kernel, count),
        [VMEM],
        jax.ShapeDtypeStruct((2, count, lane_blocks, tall, LANES), F32),
        [pltpu.VMEM((2 * count, lane_blocks, tall, LANES), F32)],
        "coefficients",
        0,
        8 * 1024 * 1024,
    )(specimen)

    outer = call(
        functools.partial(outer_kernel, height, count, width),
        [SMEM] + [VMEM] * 5 + [ANY],
        jax.ShapeDtypeStruct((4 * width + SCALE_ROWS, length), BF16),
        working(6 * width, True),
        "slices_outer_rows",
        *slice_cost(6 * width),
    )(edge, late_field, above, below, phase_index, absorption, coefficients)

    outer = lax.ppermute(outer, "depth", to_next)

    pieces = call(
        functools.partial(rows_kernel, height, width),
        [VMEM] * 4,
        jax.ShapeDtypeStruct((slabs, tall + SCALE_ROWS, 2 * height), BF16),
        [
            pltpu.VMEM((2 * height, length), F32),
            pltpu.VMEM((length + 2 * width, 2 * height), F32),
        ],
        "gap_along_rows",
        gap_flops,
        8 * 1024 * 1024,
    )(inner, outer, *tables_interleaved)
    blocks = in_lane_blocks(to_others(pieces))

    pieces = call(
        functools.partial(second_kernel, height, count, width),
        [SMEM] + [VMEM] * 4,
        jax.ShapeDtypeStruct((slabs, height + SCALE_ROWS, 2 * height), BF16),
        working(tall, False),
        "gap_slices_gap_columns",
        *slice_cost(tall),
    )(edge, blocks, coefficients, *tables_interleaved)

    blocks = in_lane_blocks(to_others(pieces))

    field = call(
        functools.partial(third_kernel, height),
        [VMEM] * 3,
        jax.ShapeDtypeStruct((2, height, length), F32),
        [],
        "gap_rows",
        gap_flops,
        6 * 1024 * 1024,
    )(blocks, *tables)
    return field[None]


def solution(mesh):
    placed = (P("depth", None, "rows", None), P("depth", "rows", None), P("depth", "rows", None))
    return jax.shard_map(
        local, mesh=mesh, in_specs=placed, out_specs=P("depth", None, "rows", None), check_vma=False
    )
```

```python
import functools
import math

import jax
import jax.numpy as jnp
import ml_dtypes
import numpy as np
from jax import lax
from jax.experimental import pallas as pl
from jax.experimental.pallas import tpu as pltpu
from jax.sharding import PartitionSpec as P

TAYLOR = 4
LATERAL = 0.22
CONTRAST = 0.2
LANES = 128
VMEM_BYTES = 24 * 1024 * 1024
ALL_VMEM_BYTES = 60 * 1024 * 1024
F32 = jnp.float32
BF16 = jnp.bfloat16


def circulant_split(column):
    length = column.shape[0]
    half = length // 2
    lag = np.arange(half)[:, None] - np.arange(half)[None, :]
    near, far = column[lag % length], column[(lag + half) % length]
    return (near + far) / 2, (near - far) / 2


def interleave(length):
    return np.arange(length).reshape(-1, LANES, 2).transpose(0, 2, 1).reshape(-1)


def gap_tables(length, interleaved):
    frequency = np.arange(length)
    frequency = np.where(frequency < length // 2, frequency, frequency - length)
    response = np.exp(-1j * math.pi * (frequency * frequency % (8 * length)) / (4 * length))
    even, odd = circulant_split(np.fft.ifft(response))
    parts = []
    for blocks in (circulant_split(even[:, 0]), (odd,)):
        table = np.stack([t for block in blocks for t in (block.real, block.imag)])
        if interleaved:
            table = table[:, :, interleave(table.shape[2])]
        table = table.astype(np.float32)
        high = table.astype(ml_dtypes.bfloat16)
        low = (table - high.astype(np.float32)).astype(ml_dtypes.bfloat16)
        parts.append(jnp.asarray(np.stack([high, low])))
    return parts


FLOOR = 255.0
SPAN = 250.0
STEEP = SPAN / math.log2(1.0 + FLOOR)
SCALE_ROWS = 16


def scale_of(arrays):
    largest = functools.reduce(jnp.maximum, [jnp.max(jnp.abs(array)) for array in arrays])
    return jnp.maximum(largest * (1.0 + 2.0**-7), 1e-30).astype(BF16).astype(F32)


def encode(values, scale):
    level = jnp.log2(1.0 + jnp.abs(values) * (FLOOR / scale))
    code = jnp.exp2(level * STEEP - SPAN / 2)
    return jnp.where(values < 0, -code, code).astype(BF16)


def decode(codes, scale):
    codes = codes.astype(F32)
    level = (jnp.log2(jnp.abs(codes)) + SPAN / 2) * (1.0 / STEEP)
    values = (jnp.exp2(level) - 1.0) * (scale * (1.0 / FLOOR))
    return jnp.where(codes < 0, -values, values)


def decode_block(blocks_ref, i, lane, rows):
    lanes = slice(lane, lane + LANES)
    scale = blocks_ref[i, rows : rows + SCALE_ROWS, lanes].astype(F32)[0:1]
    return decode(blocks_ref[i, 0:rows, lanes], scale)


def split(values):
    high = values.astype(BF16)
    return high, (values - high.astype(F32)).astype(BF16)


def product(tables, which, operand, transposed):
    high, low = operand

    def dot(part, data):
        table = tables[part, which]
        if transposed:
            return lax.dot_general(table, data, (((1,), (1,)), ((), ())), preferred_element_type=F32)
        return lax.dot_general(data, table, (((1,), (0,)), ((), ())), preferred_element_type=F32)

    return dot(0, high) + (dot(1, high) + dot(0, low))


def half_gap(tables, first, stacked, rows, transposed):
    operand = split(stacked)
    by_re = product(tables, first, operand, transposed)
    by_im = product(tables, first + 1, operand, transposed)
    if transposed:
        return (by_re[:, :rows] - by_im[:, rows:], by_re[:, rows:] + by_im[:, :rows])
    return (by_re[:rows] - by_im[rows:], by_re[rows:] + by_im[:rows])


def gap_of_parts(tables, even, odd, rows, transposed):
    small, large = tables
    quarter = even.shape[1] // 2
    left, right = even[:, :quarter], even[:, quarter:]
    sums = half_gap(small, 0, left + right, rows, transposed)
    differences = half_gap(small, 2, left - right, rows, transposed)
    axis = 0 if transposed else 1
    even = [
        jnp.concatenate([x + y, x - y], axis=axis) for x, y in zip(sums, differences, strict=True)
    ]
    odd = half_gap(large, 0, odd, rows, transposed)
    return [(even[0] + odd[0], even[1] + odd[1]), (even[0] - odd[0], even[1] - odd[1])]


def gap_transposed(tables, field, rows):
    half = field.shape[1] // 2
    left, right = field[:, :half], field[:, half:]
    return gap_of_parts(tables, left + right, left - right, rows, True)


def gap_from_blocks(tables, blocks_ref, rows):
    count = blocks_ref.shape[0] // 2

    parts = [
        [decode_block(blocks_ref, i, lane, rows) for i in range(2 * count)] for lane in (0, LANES)
    ]

    def folded(sign):
        return jnp.concatenate(
            [
                jnp.concatenate([part[i] + sign * part[i + count] for i in range(count)], axis=1)
                for part in parts
            ],
            axis=0,
        )

    return gap_of_parts(tables, folded(1.0), folded(-1.0), rows, False)


def shifted(row):
    lane = lax.broadcasted_iota(jnp.int32, row[0].shape, 1)
    count = len(row)
    moved_right = [pltpu.roll(row[i], 1, 1) for i in range(1, count, 2)]
    moved_left = [pltpu.roll(row[i], LANES - 1, 1) for i in range(0, count, 2)]
    before, after = [], []
    for i in range(count // 2):
        outside = moved_right[i - 1] if i else 0.0
        before += [jnp.where(lane == 0, outside, moved_right[i]), row[2 * i]]
        outside = moved_left[i + 1] if 2 * i + 2 < count else 0.0
        after += [row[2 * i + 1], jnp.where(lane == LANES - 1, outside, moved_left[i])]
    return before, after


def spread_rows(natural, target, first):
    blocks, tall, _ = natural.shape
    steps = tall // 8
    for i in range(blocks):
        for k in range(steps):
            target[i, 8 * (k + first) : 8 * (k + first) + 8, :] = natural.at[i][
                pl.ds(k, 8, stride=steps), :
            ]


def gather_rows(source, first, natural):
    blocks, tall, _ = natural.shape
    steps = tall // 8
    for i in range(blocks):
        for k in range(steps):
            natural.at[i][pl.ds(k, 8, stride=steps), :] = source[
                i, 8 * (k + first) : 8 * (k + first) + 8, :
            ]


def wrap(buf, steps):
    for part in range(2):
        for i in range(buf.shape[1]):
            last = buf[part, i, 8 * steps : 8 * steps + 8, :]
            buf[part, i, 0:8, :] = pltpu.roll(last, 1, 0)
            initial = buf[part, i, 8:16, :]
            buf[part, i, 8 * steps + 8 : 8 * steps + 16, :] = pltpu.roll(initial, 7, 0)


def apply_slices(count, width, inside, bufs, phase, loss, keep):
    _, blocks, tall, _ = phase.shape
    steps = tall // 8
    sublane = lax.broadcasted_iota(jnp.int32, (8, LANES), 0)
    for k in range(steps if inside else 0):
        row = sublane * steps + k
        top = jnp.logical_and(row < width, inside[0] == 0)
        bottom = jnp.logical_and(row >= tall - width, inside[1] == 0)
        keep[8 * k : 8 * k + 8, :] = jnp.where(jnp.logical_or(top, bottom), 0.0, 1.0)
    base = bufs[0]

    def step(slice_index, source, target, weight):
        def body(k):
            def rows(ref, at, *lead):
                start = (k + at) * 8
                return [ref[lead + (i, pl.ds(start, 8), slice(None))] for i in range(blocks)]

            factor = keep[pl.ds(k * 8, 8), :] * weight if inside else weight
            phases = rows(phase, 0, slice_index)
            losses = rows(loss, 0, slice_index)
            here, total = [], []
            for part in range(2):
                cells = rows(source, 1, part)
                above, below = rows(source, 0, part), rows(source, 2, part)
                before, after = shifted(cells)
                here.append(cells)
                total.append(
                    [
                        (above[i] + below[i]) + (before[i] + after[i]) + phases[i] * cells[i]
                        for i in range(blocks)
                    ]
                )
            start = pl.ds((k + 1) * 8, 8)
            for i in range(blocks):
                target[0, i, start, :] = base[0, i, start, :] - factor * (
                    total[1][i] + losses[i] * here[0][i]
                )
                target[1, i, start, :] = base[1, i, start, :] + factor * (
                    total[0][i] - losses[i] * here[1][i]
                )

        for k in range(steps):
            body(k)
        wrap(target, steps)

    for slice_index in range(count):
        source = bufs[0]
        for degree in range(TAYLOR, 0, -1):
            target = bufs[0] if degree == 1 else bufs[1 + degree % 2]
            step(slice_index, source, target, LATERAL / degree)
            source = target


def scaled_phase(values):
    return values.astype(F32) * (CONTRAST / LATERAL) - 4.0


def scaled_loss(values):
    return values.astype(F32) * (CONTRAST / LATERAL)


def by_blocks(target, start, values):
    rows = values.shape[0]
    for i in range(values.shape[1] // LANES):
        target[i, start : start + rows, :] = values[:, i * LANES : (i + 1) * LANES]


def interleaving():
    side = 2 * LANES
    line = lax.broadcasted_iota(jnp.int32, (side, side), 0)
    place = lax.broadcasted_iota(jnp.int32, (side, side), 1)
    chosen = line == 2 * (place % LANES) + place // LANES
    return jnp.where(chosen, 1.0, 0.0).astype(BF16)


def interleaved(field, specimen):
    order = interleaving()
    side = 2 * LANES
    rows = field.shape[0] if field is not None else 0
    for first in range(0, specimen.shape[1], side):
        parts = [specimen[:, first : first + side]]
        if rows:
            rest = field[:, first : first + side]
            for _ in range(2):
                part = rest.astype(BF16)
                parts.append(part)
                rest = rest - part.astype(F32)
        lines = lax.dot_general(
            jnp.concatenate(parts, axis=0) if rows else parts[0],
            order,
            (((1,), (0,)), ((), ())),
            preferred_element_type=F32,
        )
        own = specimen.shape[0]
        cells = None
        if rows:
            high, low = (lines[own + i * rows : own + (i + 1) * rows] for i in range(2))
            cells = high + low
        yield first // LANES, cells, lines[:own]


def spread_interleaved(field, specimen, count, natural, buf, phase, loss):
    rows = specimen.shape[0] // (2 * count)
    for block, cells, lines in interleaved(field, specimen):
        blocks = pl.ds(block, 2)
        for part in range(2):
            by_blocks(natural.at[part, blocks], 0, cells[part * rows : (part + 1) * rows])
        for k in range(2 * count):
            scale = scaled_phase if k < count else scaled_loss
            by_blocks(natural.at[2 + k, blocks], 0, scale(lines[k * rows : (k + 1) * rows]))
    for part in range(2):
        spread_rows(natural.at[part], buf.at[part], 1)
    wrap(buf, rows // 8)
    for k in range(count):
        spread_rows(natural.at[2 + k], phase.at[k], 0)
        spread_rows(natural.at[2 + count + k], loss.at[k], 0)


def joined(natural, start, rows):
    return jnp.concatenate(
        [
            jnp.concatenate(
                [natural[part, i, start : start + rows, :] for i in range(natural.shape[1])], axis=1
            )
            for part in range(2)
        ],
        axis=0,
    )


def turn_kernel(
    height, count, width, field, index_ref, loss_ref, out, head, tail,
    source, turned, staged, ends, came, sent, ends_came, ends_sent,
):
    length = index_ref.shape[2]
    half = height // 2
    side = 2 * LANES
    lines = [(ref, k) for ref in (index_ref, loss_ref) for k in range(count)]
    arrivals = []
    for line, (ref, k) in enumerate(lines):
        for part in range(2):
            rows = pl.ds(part * half, half)
            arrivals.append(
                pltpu.make_async_copy(
                    ref.at[k, rows], source.at[line, rows], came.at[2 * line + part]
                )
            )
    for copy in arrivals:
        copy.start()
    end_arrivals = [
        pltpu.make_async_copy(
            field.at[:, pl.ds(end * (height - width), width)],
            ends.at[end, pl.ds(0, 2)],
            ends_came.at[end],
        )
        for end in range(2)
    ]
    for copy in end_arrivals:
        copy.start()
    margin = jnp.zeros((width, height), F32)
    departures = []
    for line in range(len(lines)):
        for copy in arrivals[2 * line : 2 * line + 2]:
            copy.wait()
        ends[0, 2 + line] = source[line, 0:16, :].astype(F32)[:width]
        ends[1, 2 + line] = source[line, height - 16 :, :].astype(F32)[16 - width :]
        turned[line, 0:width, :] = margin
        turned[line, width + length :, :] = margin
        for start in range(0, length, side):
            turned[line, width + start : width + start + side, :] = (
                source[line, :, start : start + side].astype(F32).T
            )
        for k in range(out.shape[0]):
            window = turned[line, k * height : k * height + height + 2 * width, :]
            staged[line, k] = window.astype(BF16)
        departures.append(pltpu.make_async_copy(staged.at[line], out.at[:, line], sent.at[line]))
        departures[-1].start()
    for end, target in enumerate((head, tail)):
        end_arrivals[end].wait()
        departures.append(pltpu.make_async_copy(ends.at[end], target, ends_sent.at[end]))
        departures[-1].start()
    for copy in departures:
        copy.wait()


def put_coded(out, first, natural, rows, scale):
    start, stop = rows
    for i in range(natural.shape[0]):
        out[first : first + stop - start, i * LANES : (i + 1) * LANES] = encode(
            natural[i, start:stop, :], scale
        )


def put_scale(out, first, scale):
    out[first : first + SCALE_ROWS, :] = jnp.broadcast_to(
        scale, (SCALE_ROWS, out.shape[1])
    ).astype(BF16)


def inner_kernel(
    height, count, width, field, index_ref, loss_ref, out, scale_out,
    buf0, buf1, buf2, phase, loss, keep, natural,
):
    bufs = (buf0, buf1, buf2)
    length = field.shape[2]
    specimen = [ref[...].reshape(count * height, length) for ref in (index_ref, loss_ref)]
    spread_interleaved(
        field[...].reshape(2 * height, length),
        jnp.concatenate(specimen, axis=0),
        count, natural, buf0, phase, loss,
    )
    apply_slices(count, width, None, bufs, phase, loss, keep)
    for part in range(2):
        gather_rows(buf0.at[part], 1, natural.at[part])
    rows = (width, height - width)
    inner = height - 2 * width
    scale = scale_of([natural[part, :, width : height - width, :] for part in range(2)])
    for part in range(2):
        put_coded(out, part * inner, natural.at[part], rows, scale)
    scale_out[...] = jnp.broadcast_to(scale, scale_out.shape)


def outer_kernel(
    height, count, width, edge_ref, field, above, below, index_ref, loss_ref, inner_scale, ready, out,
    buf0, buf1, buf2, phase, loss, keep, natural,
):
    del ready
    bufs = (buf0, buf1, buf2)
    own = 2 * width

    def around(line, source, k):
        lines = [above[line], source[k, 0:own, :], source[k, height - own :, :], below[line]]
        return [part.astype(F32) for part in lines]

    cells = around(0, field, 0) + around(1, field, 1)
    specimen = []
    for which, source in enumerate((index_ref, loss_ref)):
        for k in range(count):
            specimen += around(2 + which * count + k, source, k)
    spread_interleaved(
        jnp.concatenate(cells, axis=0),
        jnp.concatenate(specimen, axis=0).astype(BF16),
        count, natural, buf0, phase, loss,
    )
    inside = (edge_ref[0], edge_ref[1])
    apply_slices(count, width, inside, bufs, phase, loss, keep)
    for part in range(2):
        gather_rows(buf0.at[part], 1, natural.at[part])
    ends = ((width, 2 * width), (4 * width, 5 * width))
    scale = scale_of([natural[part, :, s:e, :] for part in range(2) for s, e in ends])
    for part in range(2):
        for i in range(natural.shape[1]):
            both = jnp.concatenate([natural[part, i, s:e, :] for s, e in ends], axis=0)
            out[part * own : (part + 1) * own, i * LANES : (i + 1) * LANES] = encode(both, scale)
    put_scale(out, 2 * own, scale)
    put_scale(out, 2 * own + SCALE_ROWS, inner_scale[0:1, 0:1])


def rows_kernel(
    height, width, inner_ref, outer_ref, small, large, out, field, spectrum
):
    tables = (small, large)
    length = inner_ref.shape[1]
    inner = height - 2 * width

    def scale_in(ref, row):
        return ref[row : row + SCALE_ROWS, :].astype(F32)[0:1]

    outer_scale = scale_in(outer_ref, 4 * width)
    inner_scale = scale_in(outer_ref, 4 * width + SCALE_ROWS)
    for part in range(2):
        start = part * height
        ends = decode(outer_ref[2 * part * width : 2 * (part + 1) * width, :], outer_scale)
        field[start : start + width, :] = ends[:width]
        field[start + height - width : start + height, :] = ends[width:]
        for row in range(0, inner, 16):
            field[start + width + row : start + width + row + 16, :] = decode(
                inner_ref[part * inner + row : part * inner + row + 16, :], inner_scale
            )
    halves = gap_transposed(tables, field[...], height)
    half = length // 2
    spectrum[0:width, :] = jnp.zeros((width, 2 * height), F32)
    spectrum[width + length :, :] = jnp.zeros((width, 2 * height), F32)
    for which, (real, imag) in enumerate(halves):
        start = width + which * half
        spectrum[start : start + half, :height] = real
        spectrum[start : start + half, height:] = imag
    scale = scale_of([part for pair in halves for part in pair])
    tall = height + 2 * width
    for k in range(out.shape[0]):
        out[k, 0:tall, :] = encode(spectrum[k * height : k * height + tall, :], scale)
        put_scale(out.at[k], tall, scale)


def coefficients_kernel(count, specimen, out, natural):
    tall = natural.shape[2]
    lines = jnp.concatenate(
        [specimen[i].reshape(2 * count * tall, LANES) for i in range(specimen.shape[0])], axis=1
    )
    for block, _, cells in interleaved(None, lines):
        for k in range(2 * count):
            scale = scaled_phase if k < count else scaled_loss
            part = scale(cells[k * tall : (k + 1) * tall])
            by_blocks(natural.at[k, pl.ds(block, 2)], 0, part)
    for k in range(2 * count):
        spread_rows(natural.at[k], out.at[k // count, k % count], 0)


def second_kernel(
    height, count, width, edge_ref, blocks, coefficients, small, large, out,
    buf0, buf1, buf2, keep, natural,
):
    tables = (small, large)
    bufs = (buf0, buf1, buf2)
    tall = height + 2 * width
    length = out.shape[0] * height
    half = length // 2
    for which, halves in enumerate(gap_from_blocks(tables, blocks, tall)):
        for part in range(2):
            by_blocks(natural.at[part, pl.ds(which * half // LANES, half // LANES)], 0, halves[part])
    inside = (edge_ref[0], edge_ref[1])
    for part in range(2):
        for i in range(natural.shape[1]):
            for end, rows in enumerate((slice(0, width), slice(tall - width, tall))):
                line = natural[part, i, rows, :]
                natural[part, i, rows, :] = jnp.where(inside[end] > 0, line, 0.0)
        spread_rows(natural.at[part], buf0.at[part], 1)
    wrap(buf0, tall // 8)
    apply_slices(count, width, inside, bufs, coefficients.at[0], coefficients.at[1], keep)
    for part in range(2):
        gather_rows(buf0.at[part], 1, natural.at[part])
    halves = gap_transposed(tables, joined(natural, width, height), height)
    scale = scale_of([part for pair in halves for part in pair])
    rows_of_half = out.shape[0] // 2
    for which, (real, imag) in enumerate(halves):
        for k in range(rows_of_half):
            rows = slice(k * height, (k + 1) * height)
            target = which * rows_of_half + k
            out[target, 0:height, :height] = encode(real[rows], scale)
            out[target, 0:height, height:] = encode(imag[rows], scale)
            put_scale(out.at[target], height, scale)


def third_kernel(height, blocks, small, large, out):
    half = out.shape[2] // 2
    halves = gap_from_blocks((small, large), blocks, height)
    for which, (real, imag) in enumerate(halves):
        out[0, :, which * half : (which + 1) * half] = real
        out[1, :, which * half : (which + 1) * half] = imag


VMEM = pl.BlockSpec(memory_space=pltpu.VMEM)
SMEM = pl.BlockSpec(memory_space=pltpu.SMEM)
ANY = pl.BlockSpec(memory_space=pl.ANY)


def call(kernel, in_specs, out_shape, scratch, name, flops, moved, outs=None, room=VMEM_BYTES):
    return pl.pallas_call(
        kernel,
        in_specs=in_specs,
        out_specs=outs or VMEM,
        out_shape=out_shape,
        scratch_shapes=scratch,
        compiler_params=pltpu.CompilerParams(vmem_limit_bytes=room),
        cost_estimate=pl.CostEstimate(flops=flops, bytes_accessed=moved, transcendentals=0),
        name=name,
    )


def in_lane_blocks(pieces):
    sources, rows, both = pieces.shape
    own = both // 2
    if own == LANES:
        return pieces
    joined = pieces.reshape(sources, rows, 2, own).transpose(1, 2, 0, 3)
    joined = joined.reshape(rows, 2, sources * own // LANES, LANES).transpose(2, 0, 1, 3)
    return joined.reshape(sources * own // LANES, rows, 2 * LANES)


def to_others(pieces):
    return lax.all_to_all(pieces, "rows", split_axis=0, concat_axis=0, tiled=True)


def local(in_flight, phase_index, absorption):
    field = in_flight[0]
    count, height, length = phase_index.shape
    slabs = lax.axis_size("rows")
    groups = lax.axis_size("depth")
    width = count * TAYLOR
    tall = height + 2 * width
    place = lax.axis_index("rows")
    edge = jnp.stack([(place > 0), (place < slabs - 1)]).astype(jnp.int32)
    tables = gap_tables(length, False)
    tables_interleaved = gap_tables(length, True)

    lane_blocks = length // LANES

    def working(rows, specimen):
        buffer = pltpu.VMEM((2, lane_blocks, rows + 16, LANES), F32)
        coefficient = pltpu.VMEM((count, lane_blocks, rows, LANES), F32)
        arrays = 2 + 2 * count if specimen else 2
        return [buffer] * 3 + [coefficient] * (2 if specimen else 0) + [
            pltpu.VMEM((rows, LANES), F32),
            pltpu.VMEM((arrays, lane_blocks, rows, LANES), F32),
        ]

    def slice_cost(rows):
        cells = count * TAYLOR * rows * length
        return 40 * cells, 32 * cells

    gap_flops = 24 * height * length * length // 2
    to_next = [(g, (g + 1) % groups) for g in range(groups)]

    line_shape = jax.ShapeDtypeStruct((2 + 2 * count, width, length), F32)
    turned, head, tail = call(
        functools.partial(turn_kernel, height, count, width),
        [ANY] * 3,
        (
            jax.ShapeDtypeStruct((slabs, 2 * count, tall, height), BF16),
            line_shape,
            line_shape,
        ),
        [
            pltpu.VMEM((2 * count, height, length), BF16),
            pltpu.VMEM((2 * count, length + 2 * width, height), F32),
            pltpu.VMEM((2 * count, slabs, tall, height), BF16),
            pltpu.VMEM((2, 2 + 2 * count, width, length), F32),
            pltpu.SemaphoreType.DMA((4 * count,)),
            pltpu.SemaphoreType.DMA((2 * count,)),
            pltpu.SemaphoreType.DMA((2,)),
            pltpu.SemaphoreType.DMA((2,)),
        ],
        "specimen_columns",
        0,
        0,
        outs=(ANY, ANY, ANY),
        room=ALL_VMEM_BYTES,
    )(field, phase_index, absorption)
    turned, field = lax.optimization_barrier((turned, field))
    specimen = to_others(turned)

    inner, inner_scale = call(
        functools.partial(inner_kernel, height, count, width),
        [VMEM] * 3,
        (
            jax.ShapeDtypeStruct((2 * (height - 2 * width), length), BF16),
            jax.ShapeDtypeStruct((8, LANES), F32),
        ),
        working(height, True),
        "slices_inner_rows",
        *slice_cost(height),
        (VMEM, VMEM),
    )(field, phase_index, absorption)
    inner, head, tail = lax.optimization_barrier((inner, head, tail))
    inner = lax.ppermute(inner, "depth", to_next)
    down = [(i, i + 1) for i in range(slabs - 1)]
    up = [(i + 1, i) for i in range(slabs - 1)]
    above = lax.ppermute(tail, "rows", down)
    below = lax.ppermute(head, "rows", up)
    if height != LANES:
        specimen = specimen.transpose(1, 2, 0, 3).reshape(2 * count, tall, -1, LANES)
        specimen = specimen.transpose(2, 0, 1, 3)
    coefficients = call(
        functools.partial(coefficients_kernel, count),
        [VMEM],
        jax.ShapeDtypeStruct((2, count, lane_blocks, tall, LANES), F32),
        [pltpu.VMEM((2 * count, lane_blocks, tall, LANES), F32)],
        "coefficients",
        0,
        8 * 1024 * 1024,
    )(specimen)

    outer = call(
        functools.partial(outer_kernel, height, count, width),
        [SMEM] + [VMEM] * 6 + [ANY],
        jax.ShapeDtypeStruct((4 * width + 2 * SCALE_ROWS, length), BF16),
        working(6 * width, True),
        "slices_outer_rows",
        *slice_cost(6 * width),
    )(edge, field, above, below, phase_index, absorption, inner_scale, coefficients)

    outer = lax.ppermute(outer, "depth", to_next)

    pieces = call(
        functools.partial(rows_kernel, height, width),
        [VMEM] * 4,
        jax.ShapeDtypeStruct((slabs, tall + SCALE_ROWS, 2 * height), BF16),
        [
            pltpu.VMEM((2 * height, length), F32),
            pltpu.VMEM((length + 2 * width, 2 * height), F32),
        ],
        "gap_along_rows",
        gap_flops,
        8 * 1024 * 1024,
    )(inner, outer, *tables_interleaved)
    blocks = in_lane_blocks(to_others(pieces))

    pieces = call(
        functools.partial(second_kernel, height, count, width),
        [SMEM] + [VMEM] * 4,
        jax.ShapeDtypeStruct((slabs, height + SCALE_ROWS, 2 * height), BF16),
        working(tall, False),
        "gap_slices_gap_columns",
        *slice_cost(tall),
    )(edge, blocks, coefficients, *tables_interleaved)

    blocks = in_lane_blocks(to_others(pieces))

    field = call(
        functools.partial(third_kernel, height),
        [VMEM] * 3,
        jax.ShapeDtypeStruct((2, height, length), F32),
        [],
        "gap_rows",
        gap_flops,
        6 * 1024 * 1024,
    )(blocks, *tables)
    return field[None]


def solution(mesh):
    placed = (P("depth", None, "rows", None), P("depth", "rows", None), P("depth", "rows", None))
    return jax.shard_map(
        local, mesh=mesh, in_specs=placed, out_specs=P("depth", None, "rows", None), check_vma=False
    )
```
